128 devices in a mesh: arch: 4 (over y), clus: 32 (over x, z, core).
Axes of the slice: x: 4, y: 4, z: 4, core: 2. Of those that a mesh axis runs over, the one named last changes fastest.
Arguments:
- windows: bfloat16 [4096, 16, 3, 400], P(('arch', 'clus')), may hold values from -40 to 40
- pick_mask: int32 [4096, 16], P(('arch', 'clus')), may hold values 0 or 1
- band_member: int32 [16], replicated, may hold values 0 or 1
- event_owner: int32 [4096], replicated, may hold values from 0 to 31, as said below
- partners: int32 [4096, 32], replicated, may hold values from 0 to 4095, as said below
Outputs:
- correlation: bfloat16 [8192, 32, 16, 128], P('clus', None, 'arch')
The draws below stay inside these ranges and needn't reach their ends.
Inputs may be any that keep to these rules, and one draw needn't show every extreme that they name: `event_owner`: within each aligned block of 32 events (one archive shard), at most 2 events name the same owner, and some owner is named by exactly 2 events in every block. `partners`: every partner's owner is the event's own owner or the next one, (owner + 1) mod 32.
All inputs are finite; a program needn't handle non-finite values. No bound on the sum of `pick_mask` on one device may be relied on, other than what follows from the above.
Results may differ from the reference program's by a relative error of at most 0.0052.
Values may be sent and summed in bfloat16 or wider, within the bound.
A program may use at most 64 MiB of HBM per device.

```python
import math
import jax
import jax.numpy as jnp
from jax import lax

L = 400
COMP = 3
K = 128
K0 = 16
LAGS = 128
E_DEV = 32
NB = 32
OWNERS = 32
CAP = 2
OWN = 256
STATIONS = 16
EVENTS = 4096
ROWS = 8192
DEVICES = 128


def owner_table(key):
    pool = OWNERS * CAP
    slot_owner = jnp.arange(pool, dtype=jnp.int32) // CAP
    penalty = jax.random.randint(jax.random.fold_in(key, 11), (OWNERS,), 0, pool)
    forced = jax.random.randint(jax.random.fold_in(key, 12), (), 0, OWNERS)
    penalty = jnp.where(jnp.arange(OWNERS, dtype=jnp.int32) == forced, -2 * pool, penalty)
    block_keys = jax.random.split(jax.random.fold_in(key, 13), DEVICES)

    def one_block(block_key):
        first_key, second_key = jax.random.split(block_key)
        order = jax.random.permutation(first_key, pool).astype(jnp.int32)
        score = (order + penalty[slot_owner]) * pool + order
        chosen = slot_owner[jnp.argsort(score, stable=True)[:E_DEV]]
        return chosen[jax.random.permutation(second_key, E_DEV)]
    return jax.vmap(one_block)(block_keys).reshape(-1).astype(jnp.int32)


def draw_event_owner(key, part):
    owners = owner_table(key)
    return owners


def draw_partners(key, part):
    owners = owner_table(key)
    key = jax.random.fold_in(key, 5)
    side_key, pick_key = jax.random.split(key)
    order = jnp.argsort(owners, stable=True).astype(jnp.int32)
    counts = jnp.sum((owners[None, :] == jnp.arange(OWNERS, dtype=jnp.int32)[:, None]).astype(jnp.int32), axis=1)
    starts = jnp.cumsum(counts) - counts
    side = jax.random.randint(side_key, (EVENTS, NB), 0, 2)
    target = (owners[:, None] + side) % OWNERS
    target = jnp.where(counts[target] > 0, target, owners[:, None])
    offset = jax.random.randint(pick_key, (EVENTS, NB), 0, 1 << 20) % counts[target]
    return order[starts[target] + offset].astype(jnp.int32)


def draw_windows(key, part):
    key = jax.random.fold_in(key, 7)
    common_key, noise_key, amp_key = jax.random.split(key, 3)
    amplitude = jax.random.uniform(amp_key, (EVENTS, STATIONS, 1, 1), minval=0.5, maxval=1.5)
    rim_width = max(L // 25, 1)
    samples = jnp.arange(L, dtype=jnp.int32)
    outer = (samples < rim_width) | (samples >= L - rim_width)
    envelope = jnp.where(outer, 1.0, 0.002).astype(jnp.float32)
    common = jax.random.normal(common_key, (STATIONS, COMP, L))
    noise = jax.random.normal(noise_key, (EVENTS, STATIONS, COMP, L))
    values = (amplitude * common[None] + noise) * envelope
    return jnp.clip(values, -40.0, 40.0).astype(jnp.bfloat16)


def set_ends(array, own_key, least, largest):
    place = [jax.random.randint(jax.random.fold_in(own_key, axis), (), 0, length) for axis, length in enumerate(array.shape)]
    longest = array.shape.index(max(array.shape))
    neighbour = place[:longest] + [(place[longest] + 1) % array.shape[longest]] + place[longest + 1:]
    return array.at[tuple(place)].set(least).at[tuple(neighbour)].set(largest)


def setup_inputs(seed: int = 0) -> dict:
    keys = jax.random.split(jax.random.key(seed), 6)
    return {
        "windows": draw_windows(jax.random.fold_in(keys[5], 71), 0),
        "pick_mask": set_ends((jax.random.randint(keys[1], (EVENTS, STATIONS), 0, 4) < 3).astype(jnp.int32), jax.random.fold_in(keys[1], 1), 0, 1),
        "band_member": set_ends((jax.random.randint(keys[2], (STATIONS,), 0, 4) < 3).astype(jnp.int32), jax.random.fold_in(keys[2], 1), 0, 1),
        "event_owner": draw_event_owner(jax.random.fold_in(keys[5], 71), 0),
        "partners": draw_partners(jax.random.fold_in(keys[5], 71), 0),
    }


EPSILON = 1e-06

def forward_table():
    samples = jnp.arange(L, dtype=jnp.int32)
    bins = jnp.arange(K, dtype=jnp.int32) + K0
    turns = samples[:, None] * bins[None, :] % (2 * L)
    phase = turns.astype(jnp.float32) * (math.pi / L)
    taper = 0.5 - 0.5 * jnp.cos((samples.astype(jnp.float32) + 0.5) * (2.0 * math.pi / L))
    table = jnp.concatenate([taper[:, None] * jnp.cos(phase), -taper[:, None] * jnp.sin(phase)], axis=1)
    return table.astype(jnp.bfloat16)

def inverse_table():
    bins = jnp.arange(K, dtype=jnp.int32) + K0
    shifts = jnp.arange(LAGS, dtype=jnp.int32) - LAGS // 2
    turns = jnp.remainder(bins[:, None] * shifts[None, :], 2 * L)
    phase = turns.astype(jnp.float32) * (math.pi / L)
    return jnp.concatenate([jnp.cos(phase), -jnp.sin(phase)], axis=0).astype(jnp.bfloat16)

def transform(samples, table):
    flat = samples.reshape(-1, samples.shape[-1])
    spec = jnp.dot(flat, table, preferred_element_type=jnp.float32).astype(jnp.bfloat16)
    return spec.reshape(samples.shape[:-1] + (table.shape[1],))

def slot_layout(event_owner, device_count, block_events, owner_slots, capacity):
    blocks = event_owner.reshape(device_count, block_events)
    same_owner = blocks[:, :, None] == blocks[:, None, :]
    positions = jnp.arange(block_events, dtype=jnp.int32)
    earlier = positions[None, :] < positions[:, None]
    ranks = lax.optimization_barrier(jnp.sum((same_owner & earlier[None]).astype(jnp.int32), axis=2))
    sources = jnp.arange(device_count, dtype=jnp.int32)[:, None]
    return (blocks * owner_slots + sources * capacity + ranks).reshape(-1).astype(jnp.int32)

def correlate(near, far, near_energy, far_energy, band_scale, inverse):
    near_real = near[..., :K].astype(jnp.float32)
    near_imag = near[..., K:].astype(jnp.float32)
    far_real = far[..., :K].astype(jnp.float32)
    far_imag = far[..., K:].astype(jnp.float32)
    real_part = lax.optimization_barrier(jnp.sum(near_real * far_real + near_imag * far_imag, axis=2))
    imag_part = lax.optimization_barrier(jnp.sum(near_imag * far_real - near_real * far_imag, axis=2))
    factor = band_scale / (2.0 * COMP * K * jnp.sqrt((near_energy + EPSILON) * (far_energy + EPSILON)))
    cross = (jnp.concatenate([real_part, imag_part], axis=-1) * factor[..., None]).astype(jnp.bfloat16)
    lagged = jnp.dot(cross.reshape(-1, 2 * K), inverse, preferred_element_type=jnp.float32)
    return lagged.reshape(cross.shape[:-1] + (LAGS,)).astype(jnp.bfloat16)

def reference(windows, pick_mask, band_member, event_owner, partners):
    forward = forward_table()
    inverse = inverse_table()

    def block_spectra(pieces):
        block_windows, block_mask = pieces
        masked = block_windows * block_mask[:, :, None, None].astype(jnp.bfloat16)
        return transform(masked, forward)
    spectra = lax.map(block_spectra, (windows.reshape(DEVICES, E_DEV, STATIONS, COMP, L), pick_mask.reshape(DEVICES, E_DEV, STATIONS)))
    spectra = spectra.reshape(EVENTS, STATIONS, COMP, 2 * K)
    energy = lax.optimization_barrier(jnp.mean(jnp.square(spectra.astype(jnp.float32)), axis=(2, 3)))
    slot_rows = slot_layout(event_owner, DEVICES, E_DEV, OWN, CAP)
    slot_event = jnp.full((ROWS,), -1, jnp.int32).at[slot_rows].set(jnp.arange(EVENTS, dtype=jnp.int32))
    band_scale = band_member.astype(jnp.float32)

    def owner_block(slot_ids):
        valid = slot_ids >= 0
        safe_ids = jnp.maximum(slot_ids, 0)
        near = spectra[safe_ids]
        near_energy = energy[safe_ids]
        partner_ids = partners[safe_ids]

        def one_column(column):
            return correlate(near, spectra[column], near_energy, energy[column], band_scale, inverse)
        result = jnp.moveaxis(lax.map(one_column, partner_ids.T), 0, 1)
        return jnp.where(valid[:, None, None, None], result, jnp.zeros_like(result))
    result = lax.map(owner_block, slot_event.reshape(OWNERS, OWN))
    return result.reshape(ROWS, NB, STATIONS, LAGS)
```

```python
import functools
import math

import jax
import jax.numpy as jnp
import numpy as np
from jax import lax
from jax.experimental import pallas as pl
from jax.experimental.pallas import tpu as pltpu
from jax.sharding import PartitionSpec as P

L = 400
COMP = 3
K = 128
K0 = 16
LAGS = 128
EPSILON = 1e-06

EVENTS = 4096
BLOCK = 32
NB = 32
CAP = 2
STATIONS = 16
GROUP = 4
ROWS = COMP * GROUP * 2
TILE = GROUP * 2
PER_STEP = 8


def forward_table():
    samples = np.arange(L, dtype=np.int32)
    bins = np.arange(K, dtype=np.int32) + K0
    turns = samples[:, None] * bins[None, :] % (2 * L)
    phase = turns.astype(np.float32) * np.float32(math.pi / L)
    taper = np.float32(0.5) - np.float32(0.5) * np.cos(
        (samples.astype(np.float32) + np.float32(0.5)) * np.float32(2.0 * math.pi / L)
    )
    table = np.concatenate(
        [taper[:, None] * np.cos(phase), -taper[:, None] * np.sin(phase)], axis=1
    )
    return table.astype(jnp.bfloat16)


def inverse_table():
    bins = np.arange(K, dtype=np.int32) + K0
    shifts = np.arange(LAGS, dtype=np.int32) - LAGS // 2
    turns = np.remainder(bins[:, None] * shifts[None, :], 2 * L)
    phase = turns.astype(np.float32) * np.float32(math.pi / L)
    return np.concatenate([np.cos(phase), -np.sin(phase)], axis=0).astype(jnp.bfloat16)


def prepare_kernel(owner_ref, windows_ref, mask_ref, table_ref, out_ref, spectra, slots, counts):
    source = lax.axis_index("arch") * lax.axis_size("clus") + lax.axis_index("clus")
    owners = counts.shape[0]
    mask = mask_ref[...].astype(jnp.float32)
    table = table_ref[...]
    per = 4
    for chunk in range(BLOCK // per):
        rows = per * COMP * STATIONS
        spec = jnp.dot(
            windows_ref[chunk * rows : (chunk + 1) * rows, :],
            table,
            preferred_element_type=jnp.float32,
        )
        for e in range(per):
            event = chunk * per + e
            keep = jnp.broadcast_to(mask[:, event : event + 1], (STATIONS, K))
            for c in range(COMP):
                at = (e * COMP + c) * STATIONS
                to = (event * COMP + c) * STATIONS * 2
                spectra[pl.ds(to, STATIONS, stride=2), :] = spec[at : at + STATIONS, :K] * keep
                spectra[pl.ds(to + 1, STATIONS, stride=2), :] = spec[at : at + STATIONS, K:] * keep

    for o in range(owners):
        counts[o] = 0
        slots[2 * o] = -1
        slots[2 * o + 1] = -1

    def place(e, carry):
        owner = owner_ref[source * BLOCK + e]
        rank = counts[owner]
        slots[owner * CAP + rank] = e
        counts[owner] = rank + 1
        return carry

    lax.fori_loop(0, BLOCK, place, 0)

    def fill(o, carry):
        parts = [[], [], [], []]
        for r in range(CAP):
            e = slots[o * CAP + r]
            valid = jnp.where(e >= 0, 1.0, 0.0).astype(jnp.float32)
            base = jnp.maximum(e, 0) * (COMP * STATIONS * 2)
            for c in range(COMP):
                for a in range(STATIONS // GROUP):
                    start = pl.multiple_of(base + c * STATIONS * 2 + a * TILE, TILE)
                    parts[a].append(spectra[pl.ds(start, TILE), :] * valid)
        for a in range(STATIONS // GROUP):
            out_ref[a * owners + o] = jnp.concatenate(parts[a], axis=0).astype(jnp.bfloat16)
        return carry

    lax.fori_loop(0, owners, fill, 0)


def index_kernel(owner_ref, partners_ref, out_ref):
    mine = lax.axis_index("clus")
    own = owner_ref[...]
    lane = lax.broadcasted_iota(jnp.int32, own.shape, 1)
    inside = lane % BLOCK
    rank = jnp.zeros(own.shape, jnp.int32)
    for d in range(1, BLOCK):
        same = (pltpu.roll(own, d, 1) == own) & (inside >= d)
        rank = rank + same.astype(jnp.int32)
    row = lax.broadcasted_iota(jnp.int32, own.shape, 0)
    rank_word = jnp.sum(rank << row, axis=0, keepdims=True)
    far_word = jnp.sum((own != mine).astype(jnp.int32) << row, axis=0, keepdims=True)
    total = jnp.zeros((2 * CAP * NB, 128), jnp.float32)
    shard_of_lane = lax.broadcasted_iota(jnp.int32, (128, 128), 0) // BLOCK
    shard = lax.broadcasted_iota(jnp.int32, (128, 128), 1)
    for t in range(own.shape[0]):
        p = partners_ref[:, t * 128 : (t + 1) * 128]
        high, low = p // 128, p % 128
        parts = []
        for r in range(CAP):
            take = (own[t : t + 1, :] == mine) & (rank[t : t + 1, :] == r)
            for half in (high, low):
                parts.append(jnp.where(take, half, 0).astype(jnp.float32))
        stacked = jnp.concatenate(parts, axis=0).astype(jnp.bfloat16)
        spread = (shard_of_lane + t * (128 // BLOCK) == shard).astype(jnp.float32)
        total = total + jnp.dot(
            stacked, spread.astype(jnp.bfloat16), preferred_element_type=jnp.float32
        )
    for r in range(CAP):
        high = total[2 * r * NB : (2 * r + 1) * NB].astype(jnp.int32)
        low = total[(2 * r + 1) * NB : (2 * r + 2) * NB].astype(jnp.int32)
        rank_bits = jnp.take_along_axis(jnp.broadcast_to(rank_word, low.shape), low, axis=1)
        far_bits = jnp.take_along_axis(jnp.broadcast_to(far_word, low.shape), low, axis=1)
        rank_bit = lax.shift_right_logical(rank_bits, high) & 1
        far_bit = lax.shift_right_logical(far_bits, high) & 1
        source = high * (128 // BLOCK) + low // BLOCK
        slot = far_bit * 256 + source * CAP + rank_bit
        out_ref[r * NB : (r + 1) * NB, :] = slot


def correlate_kernel(lookup, band_ref, near_ref, far_ref, lag_ref, out_ref, table, cross_a, cross_b):
    step = pl.program_id(0)
    row = lax.broadcasted_iota(jnp.int32, (TILE, 128), 0)
    even = row % 2 == 0

    @pl.when(step == 0)
    def _():
        def normalize(ref, first):
            def one(i, carry):
                start = pl.multiple_of(i * (2 * ROWS), 2 * ROWS)
                block = ref[pl.ds(start, 2 * ROWS), :].astype(jnp.float32)
                for e in range(2):
                    parts = [
                        block[e * ROWS + c * TILE : e * ROWS + (c + 1) * TILE] for c in range(COMP)
                    ]
                    power = parts[0] * parts[0] + parts[1] * parts[1] + parts[2] * parts[2]
                    power = power + jnp.where(
                        even, pltpu.roll(power, TILE - 1, 0), pltpu.roll(power, 1, 0)
                    )
                    energy = jnp.sum(power, axis=1, keepdims=True) * (1.0 / (COMP * 2 * K))
                    scale = lax.rsqrt(energy + EPSILON)
                    for c in range(COMP):
                        to = pl.multiple_of(
                            first * ROWS + start + e * ROWS + c * TILE, TILE
                        )
                        table[pl.ds(to, TILE), :] = parts[c] * scale
                return carry

            lax.fori_loop(0, ref.shape[0] // (2 * ROWS), one, 0, unroll=4)

        normalize(near_ref, 0)
        normalize(far_ref, 256)

    band = jnp.zeros((TILE, 128), jnp.float32)
    first = lax.axis_index("arch") * GROUP
    for s in range(GROUP):
        member = band_ref[first + s].astype(jnp.float32) * (1.0 / (2.0 * COMP * K))
        band = jnp.where(row // 2 == s, member, band)
    lag = lag_ref[...]
    for i in range(PER_STEP):
        slot = step * PER_STEP + i
        shard = step * (PER_STEP // CAP) + i // CAP
        direct, turned = [], []
        for c in range(COMP):
            at = pl.multiple_of(slot * ROWS + c * TILE, TILE)
            piece = table[pl.ds(at, TILE), :] * band
            direct.append(piece)
            turned.append(
                jnp.where(even, pltpu.roll(piece, TILE - 1, 0), -pltpu.roll(piece, 1, 0))
            )
        for j in range(NB):
            base = lookup[(i % CAP) * NB + j, shard] * ROWS
            v = [table[pl.ds(pl.multiple_of(base + c * TILE, TILE), TILE), :] for c in range(COMP)]
            to = (i * NB + j) * TILE
            cross_a[to : to + TILE, :] = direct[0] * v[0] + direct[1] * v[1] + direct[2] * v[2]
            cross_b[to : to + TILE, :] = turned[0] * v[0] + turned[1] * v[1] + turned[2] * v[2]
        rows = NB * GROUP
        at = i * NB * TILE
        real = cross_a[pl.ds(at, rows, stride=2), :] + cross_a[pl.ds(at + 1, rows, stride=2), :]
        imag = cross_b[pl.ds(at, rows, stride=2), :] + cross_b[pl.ds(at + 1, rows, stride=2), :]
        cross = jnp.concatenate([real, imag], axis=1).astype(jnp.bfloat16)
        lagged = jnp.dot(cross, lag, preferred_element_type=jnp.float32)
        out_ref[i * rows : (i + 1) * rows, :] = lagged.astype(jnp.bfloat16)


def body(windows, pick_mask, band_member, event_owner, partners):
    arch_count = lax.axis_size("arch")
    clus_count = lax.axis_size("clus")
    device_count = arch_count * clus_count
    vmem = pl.BlockSpec(memory_space=pltpu.VMEM)
    smem = pl.BlockSpec(memory_space=pltpu.SMEM)
    limit = 48 * 1024 * 1024

    rows = BLOCK * COMP * STATIONS
    outgoing = pl.pallas_call(
        prepare_kernel,
        out_shape=jax.ShapeDtypeStruct((device_count, CAP * ROWS, 128), jnp.bfloat16),
        in_specs=[smem, vmem, vmem, vmem],
        out_specs=vmem,
        scratch_shapes=[
            pltpu.VMEM((rows * 2, K), jnp.float32),
            pltpu.SMEM((clus_count * CAP,), jnp.int32),
            pltpu.SMEM((clus_count,), jnp.int32),
        ],
        compiler_params=pltpu.CompilerParams(vmem_limit_bytes=limit),
        name="prepare",
    )(
        event_owner,
        jnp.transpose(windows, (0, 2, 1, 3)).reshape(rows, L),
        pick_mask.T,
        jnp.asarray(forward_table()),
    )
    lookup = pl.pallas_call(
        index_kernel,
        out_shape=jax.ShapeDtypeStruct((CAP * NB, device_count), jnp.int32),
        in_specs=[vmem, vmem],
        out_specs=vmem,
        compiler_params=pltpu.CompilerParams(vmem_limit_bytes=limit),
        name="lookup",
    )(event_owner.reshape(EVENTS // 128, 128), partners.T)

    received = lax.all_to_all(outgoing, ("arch", "clus"), split_axis=0, concat_axis=0, tiled=True)
    near = received.reshape(device_count * CAP * ROWS, 128)
    route = [((i + 1) % clus_count, i) for i in range(clus_count)]
    far = lax.ppermute(near, "clus", route)

    slots = device_count * CAP
    pair_rows = slots * NB * GROUP
    block_rows = PER_STEP * NB * GROUP
    result = pl.pallas_call(
        correlate_kernel,
        out_shape=jax.ShapeDtypeStruct((pair_rows, LAGS), jnp.bfloat16),
        grid=(slots // PER_STEP,),
        in_specs=[smem, smem, vmem, vmem, vmem],
        out_specs=pl.BlockSpec((block_rows, LAGS), lambda i: (i, 0)),
        scratch_shapes=[
            pltpu.VMEM((2 * slots * ROWS, 128), jnp.float32),
            pltpu.VMEM((PER_STEP * NB * TILE, 128), jnp.float32),
            pltpu.VMEM((PER_STEP * NB * TILE, 128), jnp.float32),
        ],
        compiler_params=pltpu.CompilerParams(vmem_limit_bytes=limit),
        name="correlate",
    )(lookup, band_member, near, far, jnp.asarray(inverse_table()))
    return result.reshape(slots, NB, GROUP, LAGS)


def solution(mesh):
    return jax.shard_map(
        body,
        mesh=mesh,
        in_specs=(P(("arch", "clus"), None, None, None), P(("arch", "clus"), None), P(), P(), P()),
        out_specs=P("clus", None, "arch", None),
        check_vma=False,
    )
```

```python
import functools
import math

import jax
import jax.numpy as jnp
import numpy as np
from jax import lax
from jax.experimental import pallas as pl
from jax.experimental.pallas import tpu as pltpu
from jax.sharding import PartitionSpec as P

L = 400
COMP = 3
K = 128
K0 = 16
LAGS = 128
EPSILON = 1e-06

EVENTS = 4096
BLOCK = 32
NB = 32
CAP = 2
STATIONS = 16
GROUP = 4
ROWS = COMP * GROUP * 2
TILE = GROUP * 2
PER_DOT = 4
PER_STEP = 8


def forward_table():
    samples = np.arange(L, dtype=np.int32)
    bins = np.arange(K, dtype=np.int32) + K0
    turns = samples[:, None] * bins[None, :] % (2 * L)
    phase = turns.astype(np.float32) * np.float32(math.pi / L)
    taper = np.float32(0.5) - np.float32(0.5) * np.cos(
        (samples.astype(np.float32) + np.float32(0.5)) * np.float32(2.0 * math.pi / L)
    )
    table = np.concatenate(
        [taper[:, None] * np.cos(phase), -taper[:, None] * np.sin(phase)], axis=1
    )
    return table.astype(jnp.bfloat16)


def inverse_table():
    bins = np.arange(K, dtype=np.int32) + K0
    shifts = np.arange(LAGS, dtype=np.int32) - LAGS // 2
    turns = np.remainder(bins[:, None] * shifts[None, :], 2 * L)
    phase = turns.astype(np.float32) * np.float32(math.pi / L)
    return np.concatenate([np.cos(phase), -np.sin(phase)], axis=0).astype(jnp.bfloat16)


def position(shard):
    y, x, z, core = shard // 32, shard // 8 % 4, shard // 2 % 4, shard % 2
    return ((z * 4 + y) * 4 + x) * 2 + core


def prepare_kernel(owner_ref, windows_ref, mask_ref, table_ref, out_ref, spectra, slots, counts):
    source = lax.axis_index("arch") * lax.axis_size("clus") + lax.axis_index("clus")
    owners = counts.shape[0]
    mask = mask_ref[...].astype(jnp.float32)
    table = table_ref[...]
    per = 4
    for chunk in range(BLOCK // per):
        rows = per * COMP * STATIONS
        spec = jnp.dot(
            windows_ref[chunk * rows : (chunk + 1) * rows, :],
            table,
            preferred_element_type=jnp.float32,
        )
        for e in range(per):
            event = chunk * per + e
            keep = jnp.broadcast_to(mask[:, event : event + 1], (STATIONS, K))
            for c in range(COMP):
                at = (e * COMP + c) * STATIONS
                to = (event * COMP + c) * STATIONS * 2
                real = spec[at : at + STATIONS, :K] * keep
                imag = spec[at : at + STATIONS, K:] * keep
                for a in range(STATIONS // GROUP):
                    some = slice(a * GROUP, (a + 1) * GROUP)
                    spectra[to + a * TILE : to + a * TILE + GROUP, :] = real[some]
                    spectra[to + a * TILE + GROUP : to + (a + 1) * TILE, :] = imag[some]

    for o in range(owners):
        counts[o] = 0
        slots[2 * o] = -1
        slots[2 * o + 1] = -1

    def place(e, carry):
        owner = owner_ref[source * BLOCK + e]
        rank = counts[owner]
        slots[owner * CAP + rank] = e
        counts[owner] = rank + 1
        return carry

    lax.fori_loop(0, BLOCK, place, 0)

    def fill(o, carry):
        parts = [[], [], [], []]
        for r in range(CAP):
            e = slots[o * CAP + r]
            valid = jnp.where(e >= 0, 1.0, 0.0).astype(jnp.float32)
            base = jnp.maximum(e, 0) * (COMP * STATIONS * 2)
            for c in range(COMP):
                for a in range(STATIONS // GROUP):
                    start = pl.multiple_of(base + c * STATIONS * 2 + a * TILE, TILE)
                    parts[a].append(spectra[pl.ds(start, TILE), :] * valid)
        for a in range(STATIONS // GROUP):
            out_ref[a * owners + o] = jnp.concatenate(parts[a], axis=0).astype(jnp.bfloat16)
        return carry

    lax.fori_loop(0, owners, fill, 0)


def index_kernel(owner_ref, partners_ref, out_ref):
    mine = lax.axis_index("clus")
    own = owner_ref[...]
    lane = lax.broadcasted_iota(jnp.int32, own.shape, 1)
    inside = lane % BLOCK
    rank = jnp.zeros(own.shape, jnp.int32)
    for d in range(1, BLOCK):
        same = (pltpu.roll(own, d, 1) == own) & (inside >= d)
        rank = rank + same.astype(jnp.int32)
    row = lax.broadcasted_iota(jnp.int32, own.shape, 0)
    rank_word = jnp.sum(rank << row, axis=0, keepdims=True)
    far_word = jnp.sum((own != mine).astype(jnp.int32) << row, axis=0, keepdims=True)
    total = jnp.zeros((2 * CAP * NB, 128), jnp.float32)
    shard_of_lane = lax.broadcasted_iota(jnp.int32, (128, 128), 0) // BLOCK
    shard = lax.broadcasted_iota(jnp.int32, (128, 128), 1)
    for t in range(own.shape[0]):
        p = partners_ref[:, t * 128 : (t + 1) * 128]
        high, low = p // 128, p % 128
        parts = []
        for r in range(CAP):
            take = (own[t : t + 1, :] == mine) & (rank[t : t + 1, :] == r)
            for half in (high, low):
                parts.append(jnp.where(take, half, 0).astype(jnp.float32))
        stacked = jnp.concatenate(parts, axis=0).astype(jnp.bfloat16)
        spread = (shard_of_lane + t * (128 // BLOCK) == shard).astype(jnp.float32)
        total = total + jnp.dot(
            stacked, spread.astype(jnp.bfloat16), preferred_element_type=jnp.float32
        )
    for r in range(CAP):
        high = total[2 * r * NB : (2 * r + 1) * NB].astype(jnp.int32)
        low = total[(2 * r + 1) * NB : (2 * r + 2) * NB].astype(jnp.int32)
        rank_bits = jnp.take_along_axis(jnp.broadcast_to(rank_word, low.shape), low, axis=1)
        far_bits = jnp.take_along_axis(jnp.broadcast_to(far_word, low.shape), low, axis=1)
        rank_bit = lax.shift_right_logical(rank_bits, high) & 1
        far_bit = lax.shift_right_logical(far_bits, high) & 1
        source = high * (128 // BLOCK) + low // BLOCK
        slot = far_bit * 256 + position(source) * CAP + rank_bit
        out_ref[r * NB : (r + 1) * NB, :] = slot * ROWS


MESH = pl.DeviceIdType.MESH
GROUPS = [(2, 2), (2, 1), (1, 2), (2, 3), (3, 2), (1, 1), (3, 3), (1, 3), (3, 1), (2, 0), (0, 2), (1, 0), (0, 1), (3, 0), (0, 3), (0, 0)]
SHARE = 8

def exchange_kernel(out_ref, own_ref, next_ref, send_sem, extra_sem, own_sem, next_sem, to_next_sem, to_own_sem, from_own_sem, from_next_sem):
    y = lax.axis_index("arch")
    me = lax.axis_index("clus")
    clus = lax.axis_size("clus")
    arch = lax.axis_size("arch")
    x, z, core = me // 8, me // 2 % 4, me % 2
    before, after = lax.rem(me + clus - 1, clus), lax.rem(me + 1, clus)
    after_z = after // 2 % 4
    after_single = x * 8 + lax.rem(z + 1, 4) * 2
    here = ((z * arch + y) * 4 + x) * 2 + core

    barrier = pltpu.get_barrier_semaphore()

    def greet(i, carry):
        other = lax.rem(y * clus + me + i, arch * clus)
        pl.semaphore_signal(barrier, inc=1, device_id=(other // clus, lax.rem(other, clus)), device_id_type=MESH)
        return carry

    lax.fori_loop(1, arch * clus, greet, 0)
    pl.semaphore_wait(barrier, arch * clus - 1)

    for dz, dy in GROUPS:
        stays = dz in (0, 3)
        buffer, sems = (own_ref, own_sem) if stays else (next_ref, next_sem)
        sem = sems.at[((0 if dz == 0 else 1) if stays else dz - 1) * 4 + dy]
        to_y, to_z = lax.rem(y + dy, arch), lax.rem(z + dz, 4)

        def send(m, carry, dz=dz, dy=dy, stays=stays, buffer=buffer, sem=sem, to_y=to_y, to_z=to_z):
            owner = lax.rem(x + m // 2, 4) * 8 + to_z * 2 + m % 2
            target = owner if stays else lax.rem(owner + clus - 1, clus)
            source = out_ref.at[to_y * clus + owner]

            def remote(done):
                pltpu.make_async_remote_copy(source, buffer.at[here], done, sem, device_id=(to_y, target), device_id_type=MESH).start()

            if dy == 0 and dz == 0:
                @pl.when(target == me)
                def _():
                    pltpu.make_async_copy(source, buffer.at[here], sem).start()

                @pl.when(target != me)
                def _():
                    remote(send_sem)
            elif dy == 0 and dz == 1:
                @pl.when(target == me)
                def _():
                    pltpu.make_async_copy(source, buffer.at[here], sem).start()

                single = (core == 0) & (owner == after_single)

                @pl.when((target != me) & single)
                def _():
                    remote(extra_sem)

                @pl.when((target != me) & jnp.logical_not(single))
                def _():
                    remote(send_sem)
            else:
                remote(send_sem)
            return carry

        lax.fori_loop(0, SHARE, send, 0)

    forwards = []
    for dz, dy in GROUPS:
        from_y = lax.rem(y - dy + arch, arch)
        if dz in (0, 3):
            k = (0 if dz == 0 else 1) * 4 + dy
            at = (lax.rem(z - dz + 4, 4) * arch + from_y) * SHARE
            block = own_ref.at[pl.ds(at, SHARE)]
            pltpu.make_async_copy(block, block, own_sem.at[k]).wait()
            copy = pltpu.make_async_remote_copy(block, next_ref.at[pl.ds(at, SHARE)], to_next_sem.at[k], from_own_sem.at[k], device_id=(y, before), device_id_type=MESH)
        else:
            k = (dz - 1) * 4 + dy
            at = (lax.rem(after_z - dz + 4, 4) * arch + from_y) * SHARE
            block = next_ref.at[pl.ds(at, SHARE)]
            pltpu.make_async_copy(block, block, next_sem.at[k]).wait()
            copy = pltpu.make_async_remote_copy(block, own_ref.at[pl.ds(at, SHARE)], to_own_sem.at[k], from_next_sem.at[k], device_id=(y, after), device_id_type=MESH)
        copy.start()
        forwards.append(copy)
    for copy in forwards:
        copy.wait()
    last = out_ref.at[pl.ds(0, arch * clus - 2)]
    pltpu.make_async_copy(last, last, send_sem).wait()

    @pl.when(core == 0)
    def _():
        one = out_ref.at[0]
        pltpu.make_async_copy(one, one, extra_sem).wait()


def correlate_kernel(lookup, band_ref, near_ref, far_ref, lag_ref, out_ref, table, *cross):
    step = pl.program_id(0)
    row = lax.broadcasted_iota(jnp.int32, (TILE, 128), 0)
    sign = jnp.where(row < GROUP, 1.0, -1.0).astype(jnp.float32)

    @pl.when(step == 0)
    def _():
        def normalize(ref, first):
            def one(i, carry):
                start = pl.multiple_of(i * (2 * ROWS), 2 * ROWS)
                block = ref[pl.ds(start, 2 * ROWS), :].astype(jnp.float32)
                for e in range(2):
                    parts = [
                        block[e * ROWS + c * TILE : e * ROWS + (c + 1) * TILE] for c in range(COMP)
                    ]
                    power = parts[0] * parts[0] + parts[1] * parts[1] + parts[2] * parts[2]
                    power = power + pltpu.roll(power, GROUP, 0)
                    energy = jnp.sum(power, axis=1, keepdims=True) * (1.0 / (COMP * 2 * K))
                    scale = lax.rsqrt(energy + EPSILON)
                    for c in range(COMP):
                        to = pl.multiple_of(first * ROWS + start + e * ROWS + c * TILE, TILE)
                        table[pl.ds(to, TILE), :] = parts[c] * scale
                return carry

            lax.fori_loop(0, ref.shape[0] // (2 * ROWS), one, 0, unroll=16)

        normalize(near_ref, 0)
        normalize(far_ref, 256)

    band = jnp.zeros((TILE, 128), jnp.float32)
    first = lax.axis_index("arch") * GROUP
    for s in range(GROUP):
        member = band_ref[first + s].astype(jnp.float32) * (1.0 / (2.0 * COMP * K))
        band = jnp.where(row % GROUP == s, member, band)
    lag = lag_ref[...]
    rows = NB * GROUP
    for i in range(0, PER_STEP, PER_DOT):
        done = []
        for d in range(PER_DOT):
            shard = step * (PER_STEP // CAP) + (i + d) // CAP
            real_r, real_i, imag_r, imag_i = [
                ref.at[(i + d) * rows : (i + d + 1) * rows] for ref in cross
            ]
            near = position(shard) * CAP + (i + d) % CAP
            direct, turned = [], []
            for c in range(COMP):
                at = pl.multiple_of(near * ROWS + c * TILE, TILE)
                piece = table[pl.ds(at, TILE), :] * band
                direct.append(piece)
                turned.append(pltpu.roll(piece, GROUP, 0) * sign)
            for j in range(NB):
                base = lookup[((i + d) % CAP) * NB + j, shard]
                v = [
                    table[pl.ds(pl.multiple_of(base + c * TILE, TILE), TILE), :]
                    for c in range(COMP)
                ]
                to = slice(j * GROUP, (j + 1) * GROUP)
                both = direct[0] * v[0] + direct[1] * v[1] + direct[2] * v[2]
                real_r[to, :] = both[:GROUP]
                real_i[to, :] = both[GROUP:]
                both = turned[0] * v[0] + turned[1] * v[1] + turned[2] * v[2]
                imag_r[to, :] = both[:GROUP]
                imag_i[to, :] = both[GROUP:]
            real = real_r[...] + real_i[...]
            imag = imag_r[...] + imag_i[...]
            done.append(jnp.concatenate([real, imag], axis=1).astype(jnp.bfloat16))
        lagged = jnp.dot(jnp.concatenate(done, axis=0), lag, preferred_element_type=jnp.float32)
        out_ref[i * rows : (i + PER_DOT) * rows, :] = lagged.astype(jnp.bfloat16)


def correlate_call(lookup, band_member, near, far):
    vmem = pl.BlockSpec(memory_space=pltpu.VMEM)
    smem = pl.BlockSpec(memory_space=pltpu.SMEM)
    limit = 48 * 1024 * 1024
    slots = near.shape[0] // ROWS
    pair_rows = slots * NB * GROUP
    block_rows = PER_STEP * NB * GROUP
    result = pl.pallas_call(
        correlate_kernel,
        out_shape=jax.ShapeDtypeStruct((pair_rows, LAGS), jnp.bfloat16),
        grid=(slots // PER_STEP,),
        in_specs=[smem, smem, vmem, vmem, vmem],
        out_specs=pl.BlockSpec((block_rows, LAGS), lambda i: (i, 0)),
        scratch_shapes=[
            pltpu.VMEM((2 * slots * ROWS, 128), jnp.float32),
            *[pltpu.VMEM((block_rows, 128), jnp.float32) for _ in range(4)],
        ],
        compiler_params=pltpu.CompilerParams(vmem_limit_bytes=limit),
        name="correlate",
    )(lookup, band_member, near, far, jnp.asarray(inverse_table()))
    return result.reshape(slots, NB, GROUP, LAGS)


def body(windows, pick_mask, band_member, event_owner, partners):
    arch_count = lax.axis_size("arch")
    clus_count = lax.axis_size("clus")
    device_count = arch_count * clus_count
    vmem = pl.BlockSpec(memory_space=pltpu.VMEM)
    smem = pl.BlockSpec(memory_space=pltpu.SMEM)
    limit = 48 * 1024 * 1024

    rows = BLOCK * COMP * STATIONS
    outgoing = pl.pallas_call(
        prepare_kernel,
        out_shape=jax.ShapeDtypeStruct((device_count, CAP * ROWS, 128), jnp.bfloat16),
        in_specs=[smem, vmem, vmem, vmem],
        out_specs=vmem,
        scratch_shapes=[
            pltpu.VMEM((rows * 2, K), jnp.float32),
            pltpu.SMEM((clus_count * CAP,), jnp.int32),
            pltpu.SMEM((clus_count,), jnp.int32),
        ],
        compiler_params=pltpu.CompilerParams(vmem_limit_bytes=limit),
        name="prepare",
    )(
        event_owner,
        jnp.transpose(windows, (0, 2, 1, 3)).reshape(rows, L),
        pick_mask.T,
        jnp.asarray(forward_table()),
    )
    lookup = pl.pallas_call(
        index_kernel,
        out_shape=jax.ShapeDtypeStruct((CAP * NB, device_count), jnp.int32),
        in_specs=[vmem, vmem],
        out_specs=vmem,
        compiler_params=pltpu.CompilerParams(vmem_limit_bytes=limit),
        name="lookup",
    )(event_owner.reshape(EVENTS // 128, 128), partners.T)

    own, following = pl.pallas_call(
        exchange_kernel,
        out_shape=[jax.ShapeDtypeStruct(outgoing.shape, outgoing.dtype)] * 2,
        in_specs=[vmem],
        out_specs=[vmem] * 2,
        scratch_shapes=[pltpu.SemaphoreType.DMA] * 2 + [pltpu.SemaphoreType.DMA((8,))] * 6,
        compiler_params=pltpu.CompilerParams(
            collective_id=0, has_side_effects=True, vmem_limit_bytes=limit
        ),
        name="exchange",
    )(outgoing)
    near = own.reshape(device_count * CAP * ROWS, 128)
    far = following.reshape(device_count * CAP * ROWS, 128)
    return correlate_call(lookup, band_member, near, far)


def solution(mesh):
    return jax.shard_map(
        body,
        mesh=mesh,
        in_specs=(P(("arch", "clus"), None, None, None), P(("arch", "clus"), None), P(), P(), P()),
        out_specs=P("clus", None, "arch", None),
        check_vma=False,
    )
```

```python
import functools
import math

import jax
import jax.numpy as jnp
import numpy as np
from jax import lax
from jax.experimental import pallas as pl
from jax.experimental.pallas import tpu as pltpu
from jax.sharding import PartitionSpec as P

L = 400
COMP = 3
K = 128
K0 = 16
LAGS = 128
EPSILON = 1e-06

EVENTS = 4096
BLOCK = 32
NB = 32
CAP = 2
STATIONS = 16
GROUP = 4
ROWS = COMP * GROUP * 2
TILE = GROUP * 2
PER_DOT = 4
PER_STEP = 32


def forward_table():
    samples = np.arange(L, dtype=np.int32)
    bins = np.arange(K, dtype=np.int32) + K0
    turns = samples[:, None] * bins[None, :] % (2 * L)
    phase = turns.astype(np.float32) * np.float32(math.pi / L)
    taper = np.float32(0.5) - np.float32(0.5) * np.cos(
        (samples.astype(np.float32) + np.float32(0.5)) * np.float32(2.0 * math.pi / L)
    )
    table = np.concatenate(
        [taper[:, None] * np.cos(phase), -taper[:, None] * np.sin(phase)], axis=1
    )
    return table.astype(jnp.bfloat16)


def inverse_table():
    bins = np.arange(K, dtype=np.int32) + K0
    shifts = np.arange(LAGS, dtype=np.int32) - LAGS // 2
    turns = np.remainder(bins[:, None] * shifts[None, :], 2 * L)
    phase = turns.astype(np.float32) * np.float32(math.pi / L)
    return np.concatenate([np.cos(phase), -np.sin(phase)], axis=0).astype(jnp.bfloat16)


def position(shard):
    y, x, z, core = shard // 32, shard // 8 % 4, shard // 2 % 4, shard % 2
    return ((z * 4 + y) * 4 + x) * 2 + core


def index_kernel(owner_ref, partners_ref, out_ref):
    mine = lax.axis_index("clus")
    own = owner_ref[...]
    lane = lax.broadcasted_iota(jnp.int32, own.shape, 1)
    inside = lane % BLOCK
    rank = jnp.zeros(own.shape, jnp.int32)
    for d in range(1, BLOCK):
        same = (pltpu.roll(own, d, 1) == own) & (inside >= d)
        rank = rank + same.astype(jnp.int32)
    row = lax.broadcasted_iota(jnp.int32, own.shape, 0)
    rank_word = jnp.sum(rank << row, axis=0, keepdims=True)
    far_word = jnp.sum((own != mine).astype(jnp.int32) << row, axis=0, keepdims=True)
    total = jnp.zeros((2 * CAP * NB, 128), jnp.float32)
    shard_of_lane = lax.broadcasted_iota(jnp.int32, (128, 128), 0) // BLOCK
    shard = lax.broadcasted_iota(jnp.int32, (128, 128), 1)
    for t in range(own.shape[0]):
        p = partners_ref[:, t * 128 : (t + 1) * 128]
        high, low = p // 128, p % 128
        parts = []
        for r in range(CAP):
            take = (own[t : t + 1, :] == mine) & (rank[t : t + 1, :] == r)
            for half in (high, low):
                parts.append(jnp.where(take, half, 0).astype(jnp.float32))
        stacked = jnp.concatenate(parts, axis=0).astype(jnp.bfloat16)
        spread = (shard_of_lane + t * (128 // BLOCK) == shard).astype(jnp.float32)
        total = total + jnp.dot(
            stacked, spread.astype(jnp.bfloat16), preferred_element_type=jnp.float32
        )
    for r in range(CAP):
        high = total[2 * r * NB : (2 * r + 1) * NB].astype(jnp.int32)
        low = total[(2 * r + 1) * NB : (2 * r + 2) * NB].astype(jnp.int32)
        rank_bits = jnp.take_along_axis(jnp.broadcast_to(rank_word, low.shape), low, axis=1)
        far_bits = jnp.take_along_axis(jnp.broadcast_to(far_word, low.shape), low, axis=1)
        rank_bit = lax.shift_right_logical(rank_bits, high) & 1
        far_bit = lax.shift_right_logical(far_bits, high) & 1
        source = high * (128 // BLOCK) + low // BLOCK
        slot = far_bit * 256 + position(source) * CAP + rank_bit
        out_ref[r * NB : (r + 1) * NB, :] = slot * ROWS


MESH = pl.DeviceIdType.MESH
GROUPS = [
    (2, 2), (2, 1), (1, 2), (2, 3), (3, 2), (1, 1), (3, 3), (1, 3),
    (3, 1), (2, 0), (0, 2), (1, 0), (0, 1), (3, 0), (0, 3), (0, 0),
]
SHARE = 8
CHUNKS = 8


def slots_of_shard(owner_ref, source, slot_ref):
    per_row = 128 // BLOCK
    own = jnp.broadcast_to(owner_ref[pl.ds(source // per_row, 1), :], (128, 128))
    row = lax.broadcasted_iota(jnp.int32, (128, 128), 0)
    lane = lax.broadcasted_iota(jnp.int32, (128, 128), 1)
    column = jnp.sum(jnp.where(row == lane, own, 0), axis=1, keepdims=True)
    earlier = (column == own) & (row // BLOCK == lane // BLOCK) & (row < lane)
    rank = jnp.sum(earlier.astype(jnp.int32), axis=0, keepdims=True)
    slot = own[:1] * CAP + rank
    slot = jnp.where(lane[:1] // BLOCK == source % per_row, slot, -1)
    count = slot_ref.shape[0]
    hit = jnp.broadcast_to(slot, (count, 128)) == row[:count]
    event = jnp.sum(jnp.where(hit, lane[:count] % BLOCK + 1, 0), axis=1, keepdims=True) - 1
    slot_ref[...] = jnp.broadcast_to(event, (count, 128))


def exchange_kernel(
    owner_ref, windows_hbm, mask_ref, forward_ref, table_ref,
    windows, spectra, out_ref, own_ref, next_ref, slot_ref, slots,
    input_sem, slot_sem, send_sem, extra_sem, own_sem, next_sem,
    to_next_sem, to_own_sem, from_own_sem, from_next_sem,
):
    y = lax.axis_index("arch")
    me = lax.axis_index("clus")
    clus = lax.axis_size("clus")
    arch = lax.axis_size("arch")
    x, z, core = me // 8, me // 2 % 4, me % 2
    before, after = lax.rem(me + clus - 1, clus), lax.rem(me + 1, clus)
    after_z = after // 2 % 4
    after_core = x * 8 + lax.rem(z + 1, 4) * 2
    here = ((z * arch + y) * 4 + x) * 2 + core
    source = y * clus + me

    part = windows.shape[0] // CHUNKS
    loads = []
    for n in range(CHUNKS):
        some = pl.ds(n * part, part)
        loads.append(
            pltpu.make_async_copy(windows_hbm.at[some], windows.at[some], input_sem.at[n])
        )
        loads[-1].start()

    barrier = pltpu.get_barrier_semaphore()

    def greet(i, carry):
        other = lax.rem(source + i, arch * clus)
        pl.semaphore_signal(
            barrier, inc=1, device_id=(other // clus, lax.rem(other, clus)), device_id_type=MESH
        )
        return carry

    lax.fori_loop(1, arch * clus, greet, 0)

    slots_of_shard(owner_ref, source, slot_ref)
    fetch = pltpu.make_async_copy(slot_ref, slots, slot_sem)
    fetch.start()

    mask = mask_ref[...].astype(jnp.float32)
    forward = forward_ref[...]
    per = BLOCK // CHUNKS
    for n in range(CHUNKS):
        loads[n].wait()
        spec = jnp.dot(
            windows[n * part : (n + 1) * part, :], forward, preferred_element_type=jnp.float32
        )
        for e in range(per):
            event = n * per + e
            keep = jnp.broadcast_to(mask[:, event : event + 1], (STATIONS, K))
            for c in range(COMP):
                at = (e * COMP + c) * STATIONS
                to = (event * COMP + c) * (STATIONS // GROUP)
                real = spec[at : at + STATIONS, :K] * keep
                imag = spec[at : at + STATIONS, K:] * keep
                for a in range(STATIONS // GROUP):
                    some = slice(a * GROUP, (a + 1) * GROUP)
                    spectra[to + a, :GROUP, :] = real[some]
                    spectra[to + a, GROUP:, :] = imag[some]
    fetch.wait()

    def fill(o, carry):
        parts = [[], [], [], []]
        for r in range(CAP):
            e = slots[o * CAP + r, 0]
            valid = jnp.where(e >= 0, 1.0, 0.0).astype(jnp.float32)
            base = jnp.maximum(e, 0) * (COMP * STATIONS // GROUP)
            for c in range(COMP):
                for a in range(STATIONS // GROUP):
                    parts[a].append(spectra[base + (c * STATIONS // GROUP + a)] * valid)
        for a in range(STATIONS // GROUP):
            out_ref[a * clus + o] = jnp.concatenate(parts[a], axis=0).astype(jnp.bfloat16)
        return carry

    lax.fori_loop(0, clus, fill, 0)
    pl.semaphore_wait(barrier, arch * clus - 1)

    def issue(dz, dy):
        stays = dz in (0, 3)
        buffer, sems = (own_ref, own_sem) if stays else (next_ref, next_sem)
        sem = sems.at[((0 if dz == 0 else 1) if stays else dz - 1) * 4 + dy]
        to_y, to_z = lax.rem(y + dy, arch), lax.rem(z + dz, 4)

        def send(m, carry):
            owner = lax.rem(x + m // 2, 4) * 8 + to_z * 2 + m % 2
            target = owner if stays else lax.rem(owner + clus - 1, clus)
            block = out_ref.at[to_y * clus + owner]

            def remote(done):
                pltpu.make_async_remote_copy(
                    block,
                    buffer.at[here],
                    done,
                    sem,
                    device_id=(to_y, target),
                    device_id_type=MESH,
                ).start()

            if dy == 0 and dz in (0, 1):
                @pl.when(target == me)
                def _():
                    pltpu.make_async_copy(block, buffer.at[here], sem).start()

                single = (core == 0) & (owner == after_core) if dz == 1 else False

                @pl.when((target != me) & single)
                def _():
                    remote(extra_sem)

                @pl.when((target != me) & jnp.logical_not(single))
                def _():
                    remote(send_sem)
            else:
                remote(send_sem)
            return carry

        lax.fori_loop(0, SHARE, send, 0)

    for dz, dy in GROUPS:
        issue(dz, dy)

    def normalize(ref, at, first):
        def one(i, carry):
            block = ref[at + i].astype(jnp.float32)
            for e in range(CAP):
                parts = [
                    block[e * ROWS + c * TILE : e * ROWS + (c + 1) * TILE] for c in range(COMP)
                ]
                power = parts[0] * parts[0] + parts[1] * parts[1] + parts[2] * parts[2]
                power = power + pltpu.roll(power, GROUP, 0)
                energy = jnp.sum(power, axis=1, keepdims=True) * (1.0 / (COMP * 2 * K))
                scale = lax.rsqrt(energy + EPSILON)
                for c in range(COMP):
                    to = (first + at + i) * (CAP * ROWS) + e * ROWS + c * TILE
                    table_ref[pl.ds(pl.multiple_of(to, TILE), TILE), :] = parts[c] * scale
            return carry

        lax.fori_loop(0, SHARE, one, 0, unroll=SHARE)

    shards = arch * clus

    def place(z_of, k):
        return (lax.rem(z_of + 4, 4) * arch + lax.rem(y - k % 4 + arch, arch)) * SHARE

    def waited(ref, sem):
        pltpu.make_async_copy(ref, ref, sem).wait()

    def pass_on(i, carry):
        k = (1 - i // 4 % 2) * 4 + (2 + 3 * i) % 4
        is_own = (i < 8) == (core == 0)

        @pl.when(is_own)
        def _():
            at = place(z + k // 4, k)
            block = own_ref.at[pl.ds(at, SHARE)]
            waited(block, own_sem.at[k])
            pltpu.make_async_remote_copy(
                block,
                next_ref.at[pl.ds(at, SHARE)],
                to_next_sem.at[k],
                from_own_sem.at[k],
                device_id=(y, before),
                device_id_type=MESH,
            ).start()
            normalize(own_ref, at, 0)

        @pl.when(jnp.logical_not(is_own))
        def _():
            at = place(after_z - 1 - k // 4, k)
            block = next_ref.at[pl.ds(at, SHARE)]
            waited(block, next_sem.at[k])
            pltpu.make_async_remote_copy(
                block,
                own_ref.at[pl.ds(at, SHARE)],
                to_own_sem.at[k],
                from_next_sem.at[k],
                device_id=(y, after),
                device_id_type=MESH,
            ).start()
            normalize(next_ref, at, shards)

        return carry

    lax.fori_loop(0, 16, pass_on, 0)

    def take(i, carry):
        k = (1 - i // 4 % 2) * 4 + (2 + 3 * i) % 4
        is_own = (i < 8) == (core == 1)

        @pl.when(is_own)
        def _():
            at = place(z - 1 - k // 4, k)
            waited(own_ref.at[pl.ds(at, SHARE)], from_next_sem.at[k])
            normalize(own_ref, at, 0)

        @pl.when(jnp.logical_not(is_own))
        def _():
            at = place(after_z + k // 4, k)
            waited(next_ref.at[pl.ds(at, SHARE)], from_own_sem.at[k])
            normalize(next_ref, at, shards)

        return carry

    lax.fori_loop(0, 16, take, 0)

    def sent(k, carry):
        waited(own_ref.at[pl.ds(0, SHARE)], to_next_sem.at[k])
        waited(next_ref.at[pl.ds(0, SHARE)], to_own_sem.at[k])
        return carry

    lax.fori_loop(0, 8, sent, 0)
    waited(out_ref.at[pl.ds(0, shards - 2)], send_sem)

    @pl.when(core == 0)
    def _():
        waited(out_ref.at[0], extra_sem)


def correlate_kernel(lookup, band_ref, table, lag_ref, out_ref):
    step = pl.program_id(0)
    row = lax.broadcasted_iota(jnp.int32, (TILE, 128), 0)
    top = row < GROUP
    sign = jnp.where(top, 1.0, -1.0).astype(jnp.float32)
    band = jnp.zeros((TILE, 128), jnp.float32)
    first = lax.axis_index("arch") * GROUP
    for s in range(GROUP):
        member = band_ref[first + s].astype(jnp.float32) * (1.0 / (2.0 * COMP * K))
        band = jnp.where(row % GROUP == s, member, band)
    lag = lag_ref[...]
    rows = NB * GROUP
    for i in range(0, PER_STEP, PER_DOT):
        pairs = []
        for d in range(PER_DOT):
            shard = step * (PER_STEP // CAP) + (i + d) // CAP
            near = position(shard) * CAP + (i + d) % CAP
            direct, turned = [], []
            for c in range(COMP):
                at = pl.multiple_of(near * ROWS + c * TILE, TILE)
                piece = table[pl.ds(at, TILE), :] * band
                direct.append(piece)
                turned.append(pltpu.roll(piece, GROUP, 0) * sign)
            for j in range(NB):
                base = lookup[((i + d) % CAP) * NB + j, shard]
                v = [
                    table[pl.ds(pl.multiple_of(base + c * TILE, TILE), TILE), :]
                    for c in range(COMP)
                ]
                real = direct[0] * v[0] + direct[1] * v[1] + direct[2] * v[2]
                imag = turned[0] * v[0] + turned[1] * v[1] + turned[2] * v[2]
                pairs.append((real, imag))
        cross = []
        for p, q in zip(pairs[::2], pairs[1::2]):
            real = jnp.concatenate([p[0], q[0]], axis=0)
            imag = jnp.concatenate([p[1], q[1]], axis=0)
            cross.append(jnp.concatenate([real, imag], axis=1).astype(jnp.bfloat16))
        wide = jnp.dot(jnp.concatenate(cross, axis=0), lag, preferred_element_type=jnp.float32)
        merged = []
        for g in range(len(cross)):
            p = wide[2 * g * TILE : (2 * g + 1) * TILE]
            q = wide[(2 * g + 1) * TILE : (2 * g + 2) * TILE]
            merged.append(jnp.where(top, p, q) + pltpu.roll(jnp.where(top, q, p), GROUP, 0))
        lagged = jnp.concatenate(merged, axis=0).astype(jnp.bfloat16)
        out_ref[i * rows : (i + PER_DOT) * rows, :] = lagged


def correlate_call(lookup, band_member, table):
    vmem = pl.BlockSpec(memory_space=pltpu.VMEM)
    smem = pl.BlockSpec(memory_space=pltpu.SMEM)
    slots = table.shape[0] // (2 * ROWS)
    pair_rows = slots * NB * GROUP
    block_rows = PER_STEP * NB * GROUP
    result = pl.pallas_call(
        correlate_kernel,
        out_shape=jax.ShapeDtypeStruct((pair_rows, LAGS), jnp.bfloat16),
        grid=(slots // PER_STEP,),
        in_specs=[smem, smem, vmem, vmem],
        out_specs=pl.BlockSpec((block_rows, LAGS), lambda i: (i, 0)),
        compiler_params=pltpu.CompilerParams(vmem_limit_bytes=24 * 1024 * 1024),
        name="correlate",
    )(lookup, band_member, table, jnp.asarray(inverse_table()))
    return result.reshape(slots, NB, GROUP, LAGS)


def body(windows, pick_mask, band_member, event_owner, partners):
    arch_count = lax.axis_size("arch")
    clus_count = lax.axis_size("clus")
    shards = arch_count * clus_count
    vmem = pl.BlockSpec(memory_space=pltpu.VMEM)
    anywhere = pl.BlockSpec(memory_space=pl.ANY)
    limit = 24 * 1024 * 1024

    rows = BLOCK * COMP * STATIONS
    owners = event_owner.reshape(EVENTS // 128, 128)
    block = pltpu.VMEM((shards, CAP * ROWS, 128), jnp.bfloat16)
    dma = pltpu.SemaphoreType.DMA
    table = pl.pallas_call(
        exchange_kernel,
        out_shape=jax.ShapeDtypeStruct((2 * shards * CAP * ROWS, 128), jnp.float32),
        in_specs=[vmem, anywhere, vmem, vmem],
        out_specs=vmem,
        scratch_shapes=[
            pltpu.VMEM((rows, L), jnp.bfloat16),
            pltpu.VMEM((rows * 2 // TILE, TILE, K), jnp.float32),
            block,
            block,
            block,
            pltpu.VMEM((clus_count * CAP, 128), jnp.int32),
            pltpu.SMEM((clus_count * CAP, 128), jnp.int32),
            dma((CHUNKS,)),
            dma,
            dma,
            dma,
        ]
        + [dma((8,))] * 6,
        compiler_params=pltpu.CompilerParams(
            collective_id=0, has_side_effects=True, vmem_limit_bytes=limit
        ),
        name="exchange",
    )(
        owners,
        jnp.transpose(windows, (0, 2, 1, 3)).reshape(rows, L),
        pick_mask.T,
        jnp.asarray(forward_table()),
    )
    lookup = pl.pallas_call(
        index_kernel,
        out_shape=jax.ShapeDtypeStruct((CAP * NB, shards), jnp.int32),
        in_specs=[vmem, vmem],
        out_specs=vmem,
        compiler_params=pltpu.CompilerParams(vmem_limit_bytes=limit),
        name="lookup",
    )(owners, partners.T)
    return correlate_call(lookup, band_member, table)


def solution(mesh):
    return jax.shard_map(
        body,
        mesh=mesh,
        in_specs=(P(("arch", "clus"), None, None, None), P(("arch", "clus"), None), P(), P(), P()),
        out_specs=P("clus", None, "arch", None),
        check_vma=False,
    )
```

```python
import functools
import math

import jax
import jax.numpy as jnp
import numpy as np
from jax import lax
from jax.experimental import pallas as pl
from jax.experimental.pallas import tpu as pltpu
from jax.sharding import PartitionSpec as P

L = 400
COMP = 3
K = 128
K0 = 16
LAGS = 128
EPSILON = 1e-06

EVENTS = 4096
BLOCK = 32
NB = 32
CAP = 2
STATIONS = 16
GROUP = 4
ROWS = COMP * GROUP * 2
TILE = GROUP * 2
PER_DOT = 4
PER_STEP = 32


def forward_table():
    samples = np.arange(L, dtype=np.int32)
    bins = np.arange(K, dtype=np.int32) + K0
    turns = samples[:, None] * bins[None, :] % (2 * L)
    phase = turns.astype(np.float32) * np.float32(math.pi / L)
    taper = np.float32(0.5) - np.float32(0.5) * np.cos(
        (samples.astype(np.float32) + np.float32(0.5)) * np.float32(2.0 * math.pi / L)
    )
    table = np.concatenate(
        [taper[:, None] * np.cos(phase), -taper[:, None] * np.sin(phase)], axis=1
    )
    return table.astype(jnp.bfloat16)


def inverse_table():
    bins = np.arange(K, dtype=np.int32) + K0
    shifts = np.arange(LAGS, dtype=np.int32) - LAGS // 2
    turns = np.remainder(bins[:, None] * shifts[None, :], 2 * L)
    phase = turns.astype(np.float32) * np.float32(math.pi / L)
    return np.concatenate([np.cos(phase), -np.sin(phase)], axis=0).astype(jnp.bfloat16)


def position(shard):
    y, x, z, core = shard // 32, shard // 8 % 4, shard // 2 % 4, shard % 2
    return ((z * 4 + y) * 4 + x) * 2 + core


def index_kernel(owner_ref, partners_ref, out_ref):
    mine = lax.axis_index("clus")
    own = owner_ref[...]
    lane = lax.broadcasted_iota(jnp.int32, own.shape, 1)
    inside = lane % BLOCK
    rank = jnp.zeros(own.shape, jnp.int32)
    for d in range(1, BLOCK):
        same = (pltpu.roll(own, d, 1) == own) & (inside >= d)
        rank = rank + same.astype(jnp.int32)
    row = lax.broadcasted_iota(jnp.int32, own.shape, 0)
    rank_word = jnp.sum(rank << row, axis=0, keepdims=True)
    far_word = jnp.sum((own != mine).astype(jnp.int32) << row, axis=0, keepdims=True)
    total = jnp.zeros((2 * CAP * NB, 128), jnp.float32)
    shard_of_lane = lax.broadcasted_iota(jnp.int32, (128, 128), 0) // BLOCK
    shard = lax.broadcasted_iota(jnp.int32, (128, 128), 1)
    for t in range(own.shape[0]):
        p = partners_ref[:, t * 128 : (t + 1) * 128]
        high, low = p // 128, p % 128
        parts = []
        for r in range(CAP):
            take = (own[t : t + 1, :] == mine) & (rank[t : t + 1, :] == r)
            for half in (high, low):
                parts.append(jnp.where(take, half, 0).astype(jnp.float32))
        stacked = jnp.concatenate(parts, axis=0).astype(jnp.bfloat16)
        spread = (shard_of_lane + t * (128 // BLOCK) == shard).astype(jnp.float32)
        total = total + jnp.dot(
            stacked, spread.astype(jnp.bfloat16), preferred_element_type=jnp.float32
        )
    for r in range(CAP):
        high = total[2 * r * NB : (2 * r + 1) * NB].astype(jnp.int32)
        low = total[(2 * r + 1) * NB : (2 * r + 2) * NB].astype(jnp.int32)
        rank_bits = jnp.take_along_axis(jnp.broadcast_to(rank_word, low.shape), low, axis=1)
        far_bits = jnp.take_along_axis(jnp.broadcast_to(far_word, low.shape), low, axis=1)
        rank_bit = lax.shift_right_logical(rank_bits, high) & 1
        far_bit = lax.shift_right_logical(far_bits, high) & 1
        source = high * (128 // BLOCK) + low // BLOCK
        slot = far_bit * 256 + position(source) * CAP + rank_bit
        out_ref[r * NB : (r + 1) * NB, :] = slot * ROWS


MESH = pl.DeviceIdType.MESH
GROUPS = [
    (2, 2), (2, 1), (1, 2), (2, 3), (3, 2), (1, 1), (3, 3), (1, 3),
    (3, 1), (2, 0), (0, 2), (1, 0), (0, 1), (3, 0), (0, 3), (0, 0),
]
SHARE = 8
CHUNKS = 8


def slots_of_shard(owner_ref, source, slot_ref):
    per_row = 128 // BLOCK
    own = jnp.broadcast_to(owner_ref[pl.ds(source // per_row, 1), :], (128, 128))
    row = lax.broadcasted_iota(jnp.int32, (128, 128), 0)
    lane = lax.broadcasted_iota(jnp.int32, (128, 128), 1)
    column = jnp.sum(jnp.where(row == lane, own, 0), axis=1, keepdims=True)
    earlier = (column == own) & (row // BLOCK == lane // BLOCK) & (row < lane)
    rank = jnp.sum(earlier.astype(jnp.int32), axis=0, keepdims=True)
    slot = own[:1] * CAP + rank
    slot = jnp.where(lane[:1] // BLOCK == source % per_row, slot, -1)
    count = slot_ref.shape[0]
    hit = jnp.broadcast_to(slot, (count, 128)) == row[:count]
    event = jnp.sum(jnp.where(hit, lane[:count] % BLOCK + 1, 0), axis=1, keepdims=True) - 1
    slot_ref[...] = jnp.broadcast_to(event, (count, 128))


def exchange_kernel(
    owner_ref, windows, mask_ref, forward_ref, table_ref,
    spectra, out_ref, own_ref, next_ref, slot_ref, slots,
    slot_sem, send_sem, extra_sem, own_sem, next_sem,
    to_next_sem, to_own_sem, from_own_sem, from_next_sem,
):
    y = lax.axis_index("arch")
    me = lax.axis_index("clus")
    clus = lax.axis_size("clus")
    arch = lax.axis_size("arch")
    x, z, core = me // 8, me // 2 % 4, me % 2
    before, after = lax.rem(me + clus - 1, clus), lax.rem(me + 1, clus)
    after_z = after // 2 % 4
    after_core = x * 8 + lax.rem(z + 1, 4) * 2
    here = ((z * arch + y) * 4 + x) * 2 + core
    source = y * clus + me

    part = windows.shape[0] // CHUNKS
    barrier = pltpu.get_barrier_semaphore()
    for dy in range(4):
        to_y = lax.rem(y + dy, arch)

        def greet(i, carry, to_y=to_y):
            to = me + i
            to = jnp.where(to >= clus, to - clus, to)
            pl.semaphore_signal(barrier, inc=1, device_id=(to_y, to), device_id_type=MESH)
            return carry

        lax.fori_loop(0 if dy else 1, clus, greet, 0, unroll=8 if dy else False)

    slots_of_shard(owner_ref, source, slot_ref)
    fetch = pltpu.make_async_copy(slot_ref, slots, slot_sem)
    fetch.start()

    mask = mask_ref[...].astype(jnp.float32)
    forward = forward_ref[...]
    per = BLOCK // CHUNKS
    for n in range(CHUNKS):
        spec = jnp.dot(
            windows[n * part : (n + 1) * part, :], forward, preferred_element_type=jnp.float32
        )
        for e in range(per):
            event = n * per + e
            keep = jnp.broadcast_to(mask[:, event : event + 1], (STATIONS, K))
            for c in range(COMP):
                at = (e * COMP + c) * STATIONS
                to = (event * COMP + c) * (STATIONS // GROUP)
                real = spec[at : at + STATIONS, :K] * keep
                imag = spec[at : at + STATIONS, K:] * keep
                for a in range(STATIONS // GROUP):
                    some = slice(a * GROUP, (a + 1) * GROUP)
                    spectra[to + a, :GROUP, :] = real[some]
                    spectra[to + a, GROUP:, :] = imag[some]
    fetch.wait()

    def fill(o, carry):
        parts = [[], [], [], []]
        for r in range(CAP):
            e = slots[o * CAP + r, 0]
            valid = jnp.where(e >= 0, 1.0, 0.0).astype(jnp.float32)
            base = jnp.maximum(e, 0) * (COMP * STATIONS // GROUP)
            for c in range(COMP):
                for a in range(STATIONS // GROUP):
                    parts[a].append(spectra[base + (c * STATIONS // GROUP + a)] * valid)
        for a in range(STATIONS // GROUP):
            out_ref[a * clus + o] = jnp.concatenate(parts[a], axis=0).astype(jnp.bfloat16)
        return carry

    lax.fori_loop(0, clus, fill, 0)
    pl.semaphore_wait(barrier, arch * clus - 1)

    def issue(owner_core, dz, dy):
        stays = dz in (0, 3)
        buffer, sems = (own_ref, own_sem) if stays else (next_ref, next_sem)
        sem = sems.at[((0 if dz == 0 else 1) if stays else dz - 1) * 4 + dy]
        to_y, to_z = lax.rem(y + dy, arch), lax.rem(z + dz, 4)

        def send(m, carry):
            owner = lax.rem(x + m, 4) * 8 + to_z * 2 + owner_core
            target = owner if stays else lax.rem(owner + clus - 1, clus)
            block = out_ref.at[to_y * clus + owner]

            def remote(done):
                pltpu.make_async_remote_copy(
                    block,
                    buffer.at[here],
                    done,
                    sem,
                    device_id=(to_y, target),
                    device_id_type=MESH,
                ).start()

            if dy == 0 and (dz == 0 or (dz == 1 and owner_core == 0)):
                @pl.when(target == me)
                def _():
                    pltpu.make_async_copy(block, buffer.at[here], sem).start()

                single = (core == 0) & (owner == after_core) if dz == 1 else False

                @pl.when((target != me) & single)
                def _():
                    remote(extra_sem)

                @pl.when((target != me) & jnp.logical_not(single))
                def _():
                    remote(send_sem)
            else:
                remote(send_sem)
            return carry

        lax.fori_loop(0, 4, send, 0)

    for owner_core in range(2):
        for dz, dy in GROUPS:
            issue(owner_core, dz, dy)

    def normalize(ref, at, first):
        def one(i, carry):
            block = ref[at + i].astype(jnp.float32)
            for e in range(CAP):
                parts = [
                    block[e * ROWS + c * TILE : e * ROWS + (c + 1) * TILE] for c in range(COMP)
                ]
                power = parts[0] * parts[0] + parts[1] * parts[1] + parts[2] * parts[2]
                power = power + pltpu.roll(power, GROUP, 0)
                energy = jnp.sum(power, axis=1, keepdims=True) * (1.0 / (COMP * 2 * K))
                scale = lax.rsqrt(energy + EPSILON)
                for c in range(COMP):
                    to = (first + at + i) * (CAP * ROWS) + e * ROWS + c * TILE
                    table_ref[pl.ds(pl.multiple_of(to, TILE), TILE), :] = parts[c] * scale
            return carry

        lax.fori_loop(0, SHARE, one, 0, unroll=SHARE)

    shards = arch * clus

    def place(z_of, k):
        return (lax.rem(z_of + 4, 4) * arch + lax.rem(y - k % 4 + arch, arch)) * SHARE

    def waited(ref, sem):
        pltpu.make_async_copy(ref, ref, sem).wait()

    own_order = [(0 if dz == 0 else 4) + dy for dz, dy in GROUPS if dz in (0, 3)]
    next_order = [(dz - 1) * 4 + dy for dz, dy in GROUPS if dz in (1, 2)]

    def pass_own():
        for k in own_order:
            at = place(z + k // 4, k)
            block = own_ref.at[pl.ds(at, SHARE)]
            waited(block, own_sem.at[k])
            pltpu.make_async_remote_copy(
                block,
                next_ref.at[pl.ds(at, SHARE)],
                to_next_sem.at[k],
                from_own_sem.at[k],
                device_id=(y, before),
                device_id_type=MESH,
            ).start()

    def pass_next():
        for k in next_order:
            at = place(after_z - 1 - k // 4, k)
            block = next_ref.at[pl.ds(at, SHARE)]
            waited(block, next_sem.at[k])
            pltpu.make_async_remote_copy(
                block,
                own_ref.at[pl.ds(at, SHARE)],
                to_own_sem.at[k],
                from_next_sem.at[k],
                device_id=(y, after),
                device_id_type=MESH,
            ).start()

    @pl.when(core == 0)
    def _():
        pass_own()
        pass_next()

    @pl.when(core == 1)
    def _():
        pass_next()
        pass_own()

    def direct(k, carry):
        normalize(own_ref, place(z + k // 4, k), 0)
        normalize(next_ref, place(after_z - 1 - k // 4, k), shards)
        return carry

    lax.fori_loop(0, 8, direct, 0)

    def take(i, carry):
        k = (1 - i // 4 % 2) * 4 + (2 + 3 * i) % 4
        is_own = (i < 8) == (core == 1)

        @pl.when(is_own)
        def _():
            at = place(z - 1 - k // 4, k)
            waited(own_ref.at[pl.ds(at, SHARE)], from_next_sem.at[k])
            normalize(own_ref, at, 0)

        @pl.when(jnp.logical_not(is_own))
        def _():
            at = place(after_z + k // 4, k)
            waited(next_ref.at[pl.ds(at, SHARE)], from_own_sem.at[k])
            normalize(next_ref, at, shards)

        return carry

    lax.fori_loop(0, 16, take, 0)

    def sent(k, carry):
        waited(own_ref.at[pl.ds(0, SHARE)], to_next_sem.at[k])
        waited(next_ref.at[pl.ds(0, SHARE)], to_own_sem.at[k])
        return carry

    lax.fori_loop(0, 8, sent, 0)
    waited(out_ref.at[pl.ds(0, shards - 2)], send_sem)

    @pl.when(core == 0)
    def _():
        waited(out_ref.at[0], extra_sem)


def correlate_kernel(lookup, band_ref, table, lag_ref, out_ref):
    step = pl.program_id(0)
    row = lax.broadcasted_iota(jnp.int32, (TILE, 128), 0)
    top = row < GROUP
    sign = jnp.where(top, 1.0, -1.0).astype(jnp.float32)
    band = jnp.zeros((TILE, 128), jnp.float32)
    first = lax.axis_index("arch") * GROUP
    for s in range(GROUP):
        member = band_ref[first + s].astype(jnp.float32) * (1.0 / (2.0 * COMP * K))
        band = jnp.where(row % GROUP == s, member, band)
    lag = lag_ref[...]
    rows = NB * GROUP
    for i in range(0, PER_STEP, PER_DOT):
        pairs = []
        for d in range(PER_DOT):
            shard = step * (PER_STEP // CAP) + (i + d) // CAP
            near = position(shard) * CAP + (i + d) % CAP
            direct, turned = [], []
            for c in range(COMP):
                at = pl.multiple_of(near * ROWS + c * TILE, TILE)
                piece = table[pl.ds(at, TILE), :] * band
                direct.append(piece)
                turned.append(pltpu.roll(piece, GROUP, 0) * sign)
            for j in range(NB):
                base = lookup[((i + d) % CAP) * NB + j, shard]
                v = [
                    table[pl.ds(pl.multiple_of(base + c * TILE, TILE), TILE), :]
                    for c in range(COMP)
                ]
                real = direct[0] * v[0] + direct[1] * v[1] + direct[2] * v[2]
                imag = turned[0] * v[0] + turned[1] * v[1] + turned[2] * v[2]
                pairs.append((real, imag))
        cross = []
        for p, q in zip(pairs[::2], pairs[1::2]):
            real = jnp.concatenate([p[0], q[0]], axis=0)
            imag = jnp.concatenate([p[1], q[1]], axis=0)
            cross.append(jnp.concatenate([real, imag], axis=1).astype(jnp.bfloat16))
        wide = jnp.dot(jnp.concatenate(cross, axis=0), lag, preferred_element_type=jnp.float32)
        merged = []
        for g in range(len(cross)):
            p = wide[2 * g * TILE : (2 * g + 1) * TILE]
            q = wide[(2 * g + 1) * TILE : (2 * g + 2) * TILE]
            merged.append(jnp.where(top, p, q) + pltpu.roll(jnp.where(top, q, p), GROUP, 0))
        lagged = jnp.concatenate(merged, axis=0).astype(jnp.bfloat16)
        out_ref[i * rows : (i + PER_DOT) * rows, :] = lagged


def correlate_call(lookup, band_member, table):
    vmem = pl.BlockSpec(memory_space=pltpu.VMEM)
    smem = pl.BlockSpec(memory_space=pltpu.SMEM)
    slots = table.shape[0] // (2 * ROWS)
    pair_rows = slots * NB * GROUP
    block_rows = PER_STEP * NB * GROUP
    result = pl.pallas_call(
        correlate_kernel,
        out_shape=jax.ShapeDtypeStruct((pair_rows, LAGS), jnp.bfloat16),
        grid=(slots // PER_STEP,),
        in_specs=[smem, smem, vmem, vmem],
        out_specs=pl.BlockSpec((block_rows, LAGS), lambda i: (i, 0)),
        compiler_params=pltpu.CompilerParams(vmem_limit_bytes=24 * 1024 * 1024),
        name="correlate",
    )(lookup, band_member, table, jnp.asarray(inverse_table()))
    return result.reshape(slots, NB, GROUP, LAGS)


def body(windows, pick_mask, band_member, event_owner, partners):
    arch_count = lax.axis_size("arch")
    clus_count = lax.axis_size("clus")
    shards = arch_count * clus_count
    vmem = pl.BlockSpec(memory_space=pltpu.VMEM)
    limit = 24 * 1024 * 1024

    rows = BLOCK * COMP * STATIONS
    owners = event_owner.reshape(EVENTS // 128, 128)
    block = pltpu.VMEM((shards, CAP * ROWS, 128), jnp.bfloat16)
    dma = pltpu.SemaphoreType.DMA
    table = pl.pallas_call(
        exchange_kernel,
        out_shape=jax.ShapeDtypeStruct((2 * shards * CAP * ROWS, 128), jnp.float32),
        in_specs=[vmem] * 4,
        out_specs=vmem,
        scratch_shapes=[
            pltpu.VMEM((rows * 2 // TILE, TILE, K), jnp.float32),
            block,
            block,
            block,
            pltpu.VMEM((clus_count * CAP, 128), jnp.int32),
            pltpu.SMEM((clus_count * CAP, 128), jnp.int32),
            dma,
            dma,
            dma,
        ]
        + [dma((8,))] * 6,
        compiler_params=pltpu.CompilerParams(
            collective_id=0, has_side_effects=True, vmem_limit_bytes=limit
        ),
        name="exchange",
    )(
        owners,
        jnp.transpose(windows, (0, 2, 1, 3)).reshape(rows, L),
        pick_mask.T,
        jnp.asarray(forward_table()),
    )
    lookup = pl.pallas_call(
        index_kernel,
        out_shape=jax.ShapeDtypeStruct((CAP * NB, shards), jnp.int32),
        in_specs=[vmem, vmem],
        out_specs=vmem,
        compiler_params=pltpu.CompilerParams(vmem_limit_bytes=limit),
        name="lookup",
    )(owners, partners.T)
    return correlate_call(lookup, band_member, table)


def solution(mesh):
    return jax.shard_map(
        body,
        mesh=mesh,
        in_specs=(P(("arch", "clus"), None, None, None), P(("arch", "clus"), None), P(), P(), P()),
        out_specs=P("clus", None, "arch", None),
        check_vma=False,
    )
```

```python
import functools
import math

import jax
import jax.numpy as jnp
import numpy as np
from jax import lax
from jax.experimental import pallas as pl
from jax.experimental.pallas import tpu as pltpu
from jax.sharding import PartitionSpec as P

L = 400
COMP = 3
K = 128
K0 = 16
LAGS = 128
EPSILON = 1e-06

EVENTS = 4096
BLOCK = 32
NB = 32
CAP = 2
STATIONS = 16
GROUP = 4
ROWS = COMP * GROUP * 2
TILE = GROUP * 2
PER_DOT = 8
PER_STEP = 64


def forward_table():
    samples = np.arange(L, dtype=np.int32)
    bins = np.arange(K, dtype=np.int32) + K0
    turns = samples[:, None] * bins[None, :] % (2 * L)
    phase = turns.astype(np.float32) * np.float32(math.pi / L)
    taper = np.float32(0.5) - np.float32(0.5) * np.cos(
        (samples.astype(np.float32) + np.float32(0.5)) * np.float32(2.0 * math.pi / L)
    )
    table = np.concatenate(
        [taper[:, None] * np.cos(phase), -taper[:, None] * np.sin(phase)], axis=1
    )
    return table.astype(jnp.bfloat16)


def inverse_table():
    bins = np.arange(K, dtype=np.int32) + K0
    shifts = np.arange(LAGS, dtype=np.int32) - LAGS // 2
    turns = np.remainder(bins[:, None] * shifts[None, :], 2 * L)
    phase = turns.astype(np.float32) * np.float32(math.pi / L)
    return np.concatenate([np.cos(phase), -np.sin(phase)], axis=0).astype(jnp.bfloat16)


def position(shard):
    y, x, z, core = shard // 32, shard // 8 % 4, shard // 2 % 4, shard % 2
    return ((z * 4 + y) * 4 + x) * 2 + core


def find_partners(mine, owner_ref, partners_ref, out_ref):
    own = owner_ref[...]
    lane = lax.broadcasted_iota(jnp.int32, own.shape, 1)
    inside = lane % BLOCK
    rank = jnp.zeros(own.shape, jnp.int32)
    for d in range(1, BLOCK):
        same = (pltpu.roll(own, d, 1) == own) & (inside >= d)
        rank = rank + same.astype(jnp.int32)
    row = lax.broadcasted_iota(jnp.int32, own.shape, 0)
    rank_word = jnp.sum(rank << row, axis=0, keepdims=True)
    far_word = jnp.sum((own != mine).astype(jnp.int32) << row, axis=0, keepdims=True)
    total = jnp.zeros((2 * CAP * NB, 128), jnp.float32)
    shard_of_lane = lax.broadcasted_iota(jnp.int32, (128, 128), 0) // BLOCK
    shard = lax.broadcasted_iota(jnp.int32, (128, 128), 1)
    for t in range(own.shape[0]):
        p = partners_ref[:, t * 128 : (t + 1) * 128]
        high, low = p // 128, p % 128
        parts = []
        for r in range(CAP):
            take = (own[t : t + 1, :] == mine) & (rank[t : t + 1, :] == r)
            for half in (high, low):
                parts.append(jnp.where(take, half, 0).astype(jnp.float32))
        stacked = jnp.concatenate(parts, axis=0).astype(jnp.bfloat16)
        spread = (shard_of_lane + t * (128 // BLOCK) == shard).astype(jnp.float32)
        total = total + jnp.dot(
            stacked, spread.astype(jnp.bfloat16), preferred_element_type=jnp.float32
        )
    for r in range(CAP):
        high = total[2 * r * NB : (2 * r + 1) * NB].astype(jnp.int32)
        low = total[(2 * r + 1) * NB : (2 * r + 2) * NB].astype(jnp.int32)
        rank_bits = jnp.take_along_axis(jnp.broadcast_to(rank_word, low.shape), low, axis=1)
        far_bits = jnp.take_along_axis(jnp.broadcast_to(far_word, low.shape), low, axis=1)
        rank_bit = lax.shift_right_logical(rank_bits, high) & 1
        far_bit = lax.shift_right_logical(far_bits, high) & 1
        source = high * (128 // BLOCK) + low // BLOCK
        slot = far_bit * 256 + position(source) * CAP + rank_bit
        out_ref[r * NB : (r + 1) * NB, :] = slot * ROWS


MESH = pl.DeviceIdType.MESH
GROUPS = [
    (2, 2), (2, 1), (1, 2), (2, 3), (3, 2), (1, 1), (3, 3), (1, 3),
    (3, 1), (2, 0), (0, 2), (1, 0), (0, 1), (3, 0), (0, 3), (0, 0),
]
SHARE = 8
CHUNKS = 8


def slots_of_shard(owner_ref, source, slot_ref):
    per_row = 128 // BLOCK
    own = jnp.broadcast_to(owner_ref[pl.ds(source // per_row, 1), :], (128, 128))
    row = lax.broadcasted_iota(jnp.int32, (128, 128), 0)
    lane = lax.broadcasted_iota(jnp.int32, (128, 128), 1)
    column = jnp.sum(jnp.where(row == lane, own, 0), axis=1, keepdims=True)
    earlier = (column == own) & (row // BLOCK == lane // BLOCK) & (row < lane)
    rank = jnp.sum(earlier.astype(jnp.int32), axis=0, keepdims=True)
    slot = own[:1] * CAP + rank
    slot = jnp.where(lane[:1] // BLOCK == source % per_row, slot, -1)
    count = slot_ref.shape[0]
    hit = jnp.broadcast_to(slot, (count, 128)) == row[:count]
    event = jnp.sum(jnp.where(hit, lane[:count] % BLOCK + 1, 0), axis=1, keepdims=True) - 1
    slot_ref[...] = jnp.broadcast_to(event, (count, 128))


def exchange_kernel(
    owner_ref, windows, mask_ref, forward_ref, partners_ref, table_ref, lookup_ref,
    lag_ref, spectra, out_ref, own_ref, next_ref, slot_ref, slots,
    slot_sem, send_sem, extra_sem, own_sem, next_sem,
    to_next_sem, to_own_sem, from_own_sem, from_next_sem,
):
    y = lax.axis_index("arch")
    me = lax.axis_index("clus")
    clus = lax.axis_size("clus")
    arch = lax.axis_size("arch")
    x, z, core = me // 8, me // 2 % 4, me % 2
    before, after = lax.rem(me + clus - 1, clus), lax.rem(me + 1, clus)
    after_z = after // 2 % 4
    after_core = x * 8 + lax.rem(z + 1, 4) * 2
    here = ((z * arch + y) * 4 + x) * 2 + core
    source = y * clus + me

    part = windows.shape[0] // CHUNKS
    barrier = pltpu.get_barrier_semaphore()
    for dy in range(4):
        to_y = lax.rem(y + dy, arch)

        def greet(i, carry, to_y=to_y):
            to = me + i
            to = jnp.where(to >= clus, to - clus, to)
            pl.semaphore_signal(barrier, inc=1, device_id=(to_y, to), device_id_type=MESH)
            return carry

        lax.fori_loop(0 if dy else 1, clus, greet, 0, unroll=8 if dy else False)

    slots_of_shard(owner_ref, source, slot_ref)
    fetch = pltpu.make_async_copy(slot_ref, slots, slot_sem)
    fetch.start()

    mask = mask_ref[...].astype(jnp.float32)
    forward = forward_ref[:L, :]
    lag_ref[:K, :] = forward_ref[L:, :LAGS]
    lag_ref[K:, :] = forward_ref[L:, LAGS:]
    per = BLOCK // CHUNKS
    for n in range(CHUNKS):
        spec = jnp.dot(
            windows[n * part : (n + 1) * part, :], forward, preferred_element_type=jnp.float32
        )
        for e in range(per):
            event = n * per + e
            keep = jnp.broadcast_to(mask[:, event : event + 1], (STATIONS, K))
            for c in range(COMP):
                at = (e * COMP + c) * STATIONS
                to = (event * COMP + c) * (STATIONS // GROUP)
                real = spec[at : at + STATIONS, :K] * keep
                imag = spec[at : at + STATIONS, K:] * keep
                for a in range(STATIONS // GROUP):
                    some = slice(a * GROUP, (a + 1) * GROUP)
                    spectra[to + a, :GROUP, :] = real[some]
                    spectra[to + a, GROUP:, :] = imag[some]
    fetch.wait()

    def fill(o, carry):
        parts = [[], [], [], []]
        for r in range(CAP):
            e = slots[o * CAP + r, 0]
            valid = jnp.where(e >= 0, 1.0, 0.0).astype(jnp.float32)
            base = jnp.maximum(e, 0) * (COMP * STATIONS // GROUP)
            for c in range(COMP):
                for a in range(STATIONS // GROUP):
                    parts[a].append(spectra[base + (c * STATIONS // GROUP + a)] * valid)
        for a in range(STATIONS // GROUP):
            out_ref[a * clus + o] = jnp.concatenate(parts[a], axis=0).astype(jnp.bfloat16)
        return carry

    lax.fori_loop(0, clus, fill, 0)
    pl.semaphore_wait(barrier, arch * clus - 1)

    def issue(owner_core, dz, dy):
        stays = dz in (0, 3)
        buffer, sems = (own_ref, own_sem) if stays else (next_ref, next_sem)
        sem = sems.at[((0 if dz == 0 else 1) if stays else dz - 1) * 4 + dy]
        to_y, to_z = lax.rem(y + dy, arch), lax.rem(z + dz, 4)

        def send(m, carry):
            owner = lax.rem(x + m, 4) * 8 + to_z * 2 + owner_core
            target = owner if stays else lax.rem(owner + clus - 1, clus)
            block = out_ref.at[to_y * clus + owner]

            def remote(done):
                pltpu.make_async_remote_copy(
                    block,
                    buffer.at[here],
                    done,
                    sem,
                    device_id=(to_y, target),
                    device_id_type=MESH,
                ).start()

            if dy == 0 and (dz == 0 or (dz == 1 and owner_core == 0)):
                @pl.when(target == me)
                def _():
                    pltpu.make_async_copy(block, buffer.at[here], sem).start()

                single = (core == 0) & (owner == after_core) if dz == 1 else False

                @pl.when((target != me) & single)
                def _():
                    remote(extra_sem)

                @pl.when((target != me) & jnp.logical_not(single))
                def _():
                    remote(send_sem)
            else:
                remote(send_sem)
            return carry

        lax.fori_loop(0, 4, send, 0)

    for owner_core in range(2):
        for dz, dy in GROUPS:
            issue(owner_core, dz, dy)

    def normalize(ref, at, first):
        def one(i, carry):
            block = ref[at + i].astype(jnp.float32)
            for e in range(CAP):
                parts = [
                    block[e * ROWS + c * TILE : e * ROWS + (c + 1) * TILE] for c in range(COMP)
                ]
                power = parts[0] * parts[0] + parts[1] * parts[1] + parts[2] * parts[2]
                power = power + pltpu.roll(power, GROUP, 0)
                energy = jnp.sum(power, axis=1, keepdims=True) * (1.0 / (COMP * 2 * K))
                scale = lax.rsqrt(energy + EPSILON)
                for c in range(COMP):
                    to = (first + at + i) * (CAP * ROWS) + e * ROWS + c * TILE
                    table_ref[pl.ds(pl.multiple_of(to, TILE), TILE), :] = parts[c] * scale
            return carry

        lax.fori_loop(0, SHARE, one, 0, unroll=SHARE)

    shards = arch * clus

    def place(z_of, k):
        return (lax.rem(z_of + 4, 4) * arch + lax.rem(y - k % 4 + arch, arch)) * SHARE

    def waited(ref, sem):
        pltpu.make_async_copy(ref, ref, sem).wait()

    own_order = [(0 if dz == 0 else 4) + dy for dz, dy in GROUPS if dz in (0, 3)]
    next_order = [(dz - 1) * 4 + dy for dz, dy in GROUPS if dz in (1, 2)]

    def pass_own():
        for k in own_order:
            at = place(z + k // 4, k)
            block = own_ref.at[pl.ds(at, SHARE)]
            waited(block, own_sem.at[k])
            pltpu.make_async_remote_copy(
                block,
                next_ref.at[pl.ds(at, SHARE)],
                to_next_sem.at[k],
                from_own_sem.at[k],
                device_id=(y, before),
                device_id_type=MESH,
            ).start()

    def pass_next():
        for k in next_order:
            at = place(after_z - 1 - k // 4, k)
            block = next_ref.at[pl.ds(at, SHARE)]
            waited(block, next_sem.at[k])
            pltpu.make_async_remote_copy(
                block,
                own_ref.at[pl.ds(at, SHARE)],
                to_own_sem.at[k],
                from_next_sem.at[k],
                device_id=(y, after),
                device_id_type=MESH,
            ).start()

    @pl.when(core == 0)
    def _():
        pass_own()
        pass_next()

    @pl.when(core == 1)
    def _():
        pass_next()
        pass_own()

    find_partners(me, owner_ref, partners_ref, lookup_ref)

    def direct(k, carry):
        normalize(own_ref, place(z + k // 4, k), 0)
        normalize(next_ref, place(after_z - 1 - k // 4, k), shards)
        return carry

    lax.fori_loop(0, 8, direct, 0)

    def take(i, carry):
        k = (1 - i // 4 % 2) * 4 + (2 + 3 * i) % 4
        is_own = (i < 8) == (core == 1)

        @pl.when(is_own)
        def _():
            at = place(z - 1 - k // 4, k)
            waited(own_ref.at[pl.ds(at, SHARE)], from_next_sem.at[k])
            normalize(own_ref, at, 0)

        @pl.when(jnp.logical_not(is_own))
        def _():
            at = place(after_z + k // 4, k)
            waited(next_ref.at[pl.ds(at, SHARE)], from_own_sem.at[k])
            normalize(next_ref, at, shards)

        return carry

    lax.fori_loop(0, 16, take, 0)

    def sent(k, carry):
        waited(own_ref.at[pl.ds(0, SHARE)], to_next_sem.at[k])
        waited(next_ref.at[pl.ds(0, SHARE)], to_own_sem.at[k])
        return carry

    lax.fori_loop(0, 8, sent, 0)
    waited(out_ref.at[pl.ds(0, shards - 2)], send_sem)

    @pl.when(core == 0)
    def _():
        waited(out_ref.at[0], extra_sem)


def correlate_kernel(lookup, band_ref, table, lag_ref, out_ref):
    step = pl.program_id(0)
    row = lax.broadcasted_iota(jnp.int32, (TILE, 128), 0)
    top = row < GROUP
    sign = jnp.where(top, 1.0, -1.0).astype(jnp.float32)
    band = jnp.zeros((TILE, 128), jnp.float32)
    first = lax.axis_index("arch") * GROUP
    for s in range(GROUP):
        member = band_ref[first + s].astype(jnp.float32) * (1.0 / (2.0 * COMP * K))
        band = jnp.where(row % GROUP == s, member, band)
    lag = lag_ref[...]
    rows = NB * GROUP
    for i in range(0, PER_STEP, PER_DOT):
        pairs = []
        for d in range(PER_DOT):
            shard = step * (PER_STEP // CAP) + (i + d) // CAP
            near = position(shard) * CAP + (i + d) % CAP
            direct, turned = [], []
            for c in range(COMP):
                at = pl.multiple_of(near * ROWS + c * TILE, TILE)
                piece = table[pl.ds(at, TILE), :] * band
                direct.append(piece)
                turned.append(pltpu.roll(piece, GROUP, 0) * sign)
            for j in range(NB):
                base = lookup[((i + d) % CAP) * NB + j, shard]
                v = [
                    table[pl.ds(pl.multiple_of(base + c * TILE, TILE), TILE), :]
                    for c in range(COMP)
                ]
                real = direct[0] * v[0] + direct[1] * v[1] + direct[2] * v[2]
                imag = turned[0] * v[0] + turned[1] * v[1] + turned[2] * v[2]
                pairs.append((real, imag))
        cross = []
        for p, q in zip(pairs[::2], pairs[1::2]):
            real = jnp.concatenate([p[0], q[0]], axis=0)
            imag = jnp.concatenate([p[1], q[1]], axis=0)
            cross.append(jnp.concatenate([real, imag], axis=1).astype(jnp.bfloat16))
        wide = jnp.dot(jnp.concatenate(cross, axis=0), lag, preferred_element_type=jnp.float32)
        merged = []
        for g in range(len(cross)):
            p = wide[2 * g * TILE : (2 * g + 1) * TILE]
            q = wide[(2 * g + 1) * TILE : (2 * g + 2) * TILE]
            merged.append(jnp.where(top, p, q) + pltpu.roll(jnp.where(top, q, p), GROUP, 0))
        lagged = jnp.concatenate(merged, axis=0).astype(jnp.bfloat16)
        out_ref[i * rows : (i + PER_DOT) * rows, :] = lagged


def correlate_call(lookup, band_member, table, lag):
    vmem = pl.BlockSpec(memory_space=pltpu.VMEM)
    smem = pl.BlockSpec(memory_space=pltpu.SMEM)
    slots = table.shape[0] // (2 * ROWS)
    pair_rows = slots * NB * GROUP
    block_rows = PER_STEP * NB * GROUP
    result = pl.pallas_call(
        correlate_kernel,
        out_shape=jax.ShapeDtypeStruct((pair_rows, LAGS), jnp.bfloat16),
        grid=(slots // PER_STEP,),
        in_specs=[smem, smem, vmem, vmem],
        out_specs=pl.BlockSpec((block_rows, LAGS), lambda i: (i, 0)),
        compiler_params=pltpu.CompilerParams(vmem_limit_bytes=24 * 1024 * 1024),
        name="correlate",
    )(lookup, band_member, table, lag)
    return result.reshape(slots, NB, GROUP, LAGS)


def body(windows, pick_mask, band_member, event_owner, partners):
    arch_count = lax.axis_size("arch")
    clus_count = lax.axis_size("clus")
    shards = arch_count * clus_count
    vmem = pl.BlockSpec(memory_space=pltpu.VMEM)
    limit = 24 * 1024 * 1024

    rows = BLOCK * COMP * STATIONS
    owners = event_owner.reshape(EVENTS // 128, 128)
    block = pltpu.VMEM((shards, CAP * ROWS, 128), jnp.bfloat16)
    dma = pltpu.SemaphoreType.DMA
    lag_rows = inverse_table()
    tables = np.concatenate(
        [forward_table(), np.concatenate([lag_rows[:K], lag_rows[K:]], axis=1)], axis=0
    )
    table, lookup, lag = pl.pallas_call(
        exchange_kernel,
        out_shape=[
            jax.ShapeDtypeStruct((2 * shards * CAP * ROWS, 128), jnp.float32),
            jax.ShapeDtypeStruct((CAP * NB, shards), jnp.int32),
            jax.ShapeDtypeStruct((2 * K, LAGS), jnp.bfloat16),
        ],
        in_specs=[vmem] * 5,
        out_specs=[vmem] * 3,
        scratch_shapes=[
            pltpu.VMEM((rows * 2 // TILE, TILE, K), jnp.float32),
            block,
            block,
            block,
            pltpu.VMEM((clus_count * CAP, 128), jnp.int32),
            pltpu.SMEM((clus_count * CAP, 128), jnp.int32),
            dma,
            dma,
            dma,
        ]
        + [dma((8,))] * 6,
        compiler_params=pltpu.CompilerParams(
            collective_id=0, has_side_effects=True, vmem_limit_bytes=limit
        ),
        name="exchange",
    )(
        owners,
        jnp.transpose(windows, (0, 2, 1, 3)).reshape(rows, L),
        pick_mask.T,
        jnp.asarray(tables),
        partners.T,
    )
    return correlate_call(lookup, band_member, table, lag)


def solution(mesh):
    return jax.shard_map(
        body,
        mesh=mesh,
        in_specs=(P(("arch", "clus"), None, None, None), P(("arch", "clus"), None), P(), P(), P()),
        out_specs=P("clus", None, "arch", None),
        check_vma=False,
    )
```
